256 devices in a mesh: seq: 16 (over z, core), chan: 16 (over x, y).
Axes of the slice: x: 4, y: 4, z: 8, core: 2. Of those that a mesh axis runs over, the one named last changes fastest.
Arguments:
- x_groups: bfloat16 [32, 128, 4096], P('seq', None, 'chan'), may hold values from -6 to 6
- grad_groups: bfloat16 [32, 128, 4096], P('seq', None, 'chan'), may hold values from -0.09375 to 0.09375
- filters: bfloat16 [4096, 4096], P('seq', 'chan'), may hold values from -6 to 6
- group_order: int32 [32], replicated, may hold values from 0 to 31, each once
Outputs:
- grad_x: bfloat16 [32, 128, 4096], P('seq', None, 'chan')
- grad_filters: float32 [4096, 4096], P('seq', 'chan')
The draws below stay inside these ranges and needn't reach their ends.
Inputs may be any that keep to these rules, and one draw needn't show every extreme that they name: `group_order`: a permutation of the 32 block numbers.
All inputs are finite; a program needn't handle non-finite values.
Results may differ from the reference program's by a relative error of at most 0.001.
Values may be sent and summed in bfloat16 or wider, within the bound.
No kernel may reach another device: no remote copies, remote signals or barrier semaphores. Data moves between devices by JAX's collectives and lax.ppermute only.
A program may use at most 128 MiB of HBM per device.

```python
import jax
import jax.numpy as jnp

C = 4096
GROUP = 128
GROUPS = 32
SEQ = 4096


def levels(stream_key, shape, cuts, least, largest):
    gain = 1.0
    for dim, parts in cuts:
        steps = jax.random.uniform(jax.random.fold_in(jax.random.fold_in(stream_key, 6), dim), (parts,), jnp.float32, least / len(cuts), largest / len(cuts))
        gain = gain * jnp.repeat(jnp.exp(steps), shape[dim] // parts).reshape((-1,) + (1,) * (len(shape) - 1 - dim))
    return gain


def noise(rng, extent, width, limit, split=(), dtype=jnp.bfloat16):
    level = levels(rng, extent, split, -0.22, 0.18) if split else 1.0
    entries = jax.random.normal(rng, extent, jnp.float32) * width * level
    return jnp.minimum(jnp.maximum(entries, -limit), limit).astype(dtype)


def setup_inputs(seed: int = 0) -> dict:
    arg_keys = jax.random.split(jax.random.key(seed), 5)
    x_groups = noise(arg_keys[0], (GROUPS, GROUP, C), 1.0, 6.0, ((0, 16), (2, 16)))
    grad_groups = noise(arg_keys[1], (GROUPS, GROUP, C), SEQ ** -0.5, 0.09375, ((0, 16), (2, 16)))
    filters = noise(arg_keys[2], (SEQ, C), 1.0, 6.0, ((0, 16), (1, 16)))
    group_order = jax.random.permutation(arg_keys[3], GROUPS).astype(jnp.int32)
    return dict(x_groups=x_groups, grad_groups=grad_groups, filters=filters, group_order=group_order)


def reference(x_groups, grad_groups, filters, group_order):
    x_seq = jnp.zeros_like(x_groups).at[group_order].set(x_groups).reshape(SEQ, C).astype(jnp.float32)
    g_seq = jnp.zeros_like(grad_groups).at[group_order].set(grad_groups).reshape(SEQ, C).astype(jnp.float32)
    h_seq = filters.astype(jnp.float32)
    length = 2 * SEQ
    spectrum = jnp.fft.rfft(g_seq, length, axis=0)
    grad_filters = jnp.fft.irfft(spectrum * jnp.conj(jnp.fft.rfft(x_seq, length, axis=0)), length, axis=0)[:SEQ]
    dx_seq = jnp.fft.irfft(spectrum * jnp.conj(jnp.fft.rfft(h_seq, length, axis=0)), length, axis=0)[:SEQ]
    grad_x = dx_seq.reshape(GROUPS, GROUP, C)[group_order].astype(jnp.bfloat16)
    return grad_x, grad_filters.astype(jnp.float32)
```

```python
import functools

import jax
import jax.numpy as jnp
from jax import lax
from jax.experimental import pallas as pl
from jax.experimental.pallas import tpu as pltpu
from jax.sharding import PartitionSpec as P

VMEM_LIMIT = 48 * 1024 * 1024


def permuter(size, flip):
    rows = lax.broadcasted_iota(jnp.int32, (size, size), 0)
    cols = lax.broadcasted_iota(jnp.int32, (size, size), 1)
    if flip:
        cols = size - 1 - cols
    return (rows == cols).astype(jnp.float32).astype(jnp.bfloat16)


def transposed(eye, value):
    return lax.dot_general(
        eye, value, (((1,), (1,)), ((), ())), preferred_element_type=jnp.float32
    )


def pack_kernel(x_hbm, g_hbm, h_hbm, out_ref, x_ref, g_ref, h_ref, sems):
    peers, _, blocks, part, rows = out_ref.shape
    channels = peers * part
    copies = [
        pltpu.make_async_copy(source, target, sems.at[i])
        for i, (source, target) in enumerate(
            ((x_hbm, x_ref), (g_hbm, g_ref), (h_hbm, h_ref))
        )
    ]
    for copy in copies:
        copy.start()
    for copy in copies:
        copy.wait()
    eye = permuter(channels, False)
    flip = permuter(rows, True)
    for b in range(blocks):
        flipped = jnp.dot(flip, g_ref[b], preferred_element_type=jnp.float32)
        for a, value in enumerate(
            (x_ref[b], flipped.astype(jnp.bfloat16), h_ref[b * rows : (b + 1) * rows, :])
        ):
            out_ref[:, a, b] = (
                transposed(eye, value).astype(jnp.bfloat16).reshape(peers, part, rows)
            )


def unpack_kernel(in_ref, gx_ref, gf_ref):
    peers, _, blocks, part, rows = in_ref.shape
    channels = peers * part
    eye = permuter(rows, True)
    for b in range(blocks):
        high = in_ref[:, 0, b].reshape(channels, rows)
        low = in_ref[:, 1, b].reshape(channels, rows)
        dx = in_ref[:, 2, b].reshape(channels, rows)
        gf_ref[b * rows : (b + 1) * rows, :] = transposed(eye, high) + transposed(eye, low)
        gx_ref[b] = transposed(eye, dx).astype(jnp.bfloat16)


def conv_kernel(order_ref, in_ref, out_ref, rev, seq, res):
    peers, _, blocks, part, rows = in_ref.shape
    total = peers * blocks
    step = 16
    f32, bf16 = jnp.float32, jnp.bfloat16
    flat = rev.reshape(2 * part * 2 * total, rows)
    for v in range(2):
        for c in range(part):
            rev[v, c, total:] = jnp.zeros((total, rows), f32)
    seq[total] = jnp.zeros((part, rows), f32)

    def put(v, place, tile):
        start = v * part * 2 * total + total - 1 - place
        flat[pl.ds(start, part, stride=2 * total), :] = tile.astype(f32)

    for j in range(total):
        place = order_ref[j]
        put(0, place, in_ref[j // blocks, 0, j % blocks])
        seq[place] = in_ref[j // blocks, 1, j % blocks].astype(f32)
        put(1, j, in_ref[j // blocks, 2, j % blocks])
    inside = lax.broadcasted_iota(jnp.int32, (rows, rows), 0) <= lax.broadcasted_iota(
        jnp.int32, (rows, rows), 1
    )

    def circulant(k, c):
        row = jnp.broadcast_to(seq[k, pl.ds(c, 1), :], (step, rows))
        base = pltpu.roll(row, 0, 1, stride=1, stride_axis=0).astype(bf16)
        tiles = [base] + [
            pltpu.roll(base, step * e, 1) for e in range(1, rows // step)
        ]
        return jnp.concatenate(tiles, axis=0)

    def channel(c, carry):
        now = circulant(0, c)
        acc = jnp.zeros((2 * total, rows), f32)
        for k in range(0, total, 2):
            tiles = []
            for i in range(2):
                after = circulant(k + i + 1, c)
                tiles.append(jnp.where(inside, now, after))
                now = after
            left = [
                jnp.concatenate(
                    [rev[v, c, total - 1 - k - i : 2 * total - 1 - k - i, :] for v in range(2)],
                    axis=0,
                ).astype(bf16)
                for i in range(2)
            ]
            acc += jnp.dot(
                jnp.concatenate(left, axis=1),
                jnp.concatenate(tiles, axis=0),
                preferred_element_type=f32,
            )
        res[c] = acc
        return carry

    lax.fori_loop(0, part, channel, 0)
    results = res.reshape(part * 2 * total, rows)
    for j in range(total):
        place = order_ref[j]
        value = results[pl.ds(j, part, stride=2 * total), :]
        dx = results[pl.ds(total + place, part, stride=2 * total), :]
        high = value.astype(bf16)
        out_ref[j // blocks, 0, j % blocks] = high
        out_ref[j // blocks, 1, j % blocks] = (value - high.astype(f32)).astype(bf16)
        out_ref[j // blocks, 2, j % blocks] = dx.astype(bf16)


def per_device(x_groups, grad_groups, filters, group_order):
    blocks, rows, channels = x_groups.shape
    peers = lax.axis_size("seq")
    part = channels // peers
    total = peers * blocks
    vmem = pl.BlockSpec(memory_space=pltpu.VMEM)
    smem = pl.BlockSpec(memory_space=pltpu.SMEM)
    params = pltpu.CompilerParams(vmem_limit_bytes=VMEM_LIMIT)
    packed = jax.ShapeDtypeStruct((peers, 3, blocks, part, rows), jnp.bfloat16)
    send = pl.pallas_call(
        pack_kernel,
        out_shape=packed,
        in_specs=[pl.BlockSpec(memory_space=pltpu.HBM)] * 3,
        out_specs=vmem,
        scratch_shapes=[
            pltpu.VMEM((blocks, rows, channels), jnp.bfloat16),
            pltpu.VMEM((blocks, rows, channels), jnp.bfloat16),
            pltpu.VMEM((blocks * rows, channels), jnp.bfloat16),
            pltpu.SemaphoreType.DMA((3,)),
        ],
        compiler_params=params,
    )(x_groups, grad_groups, filters)
    got = lax.all_to_all(send, "seq", 0, 0, tiled=True)
    back = pl.pallas_call(
        conv_kernel,
        out_shape=packed,
        in_specs=[smem, vmem],
        out_specs=vmem,
        scratch_shapes=[
            pltpu.VMEM((2, part, 2 * total, rows), jnp.float32),
            pltpu.VMEM((total + 1, part, rows), jnp.float32),
            pltpu.VMEM((part, 2 * total, rows), jnp.float32),
        ],
        compiler_params=params,
    )(group_order, got)
    home = lax.all_to_all(back, "seq", 0, 0, tiled=True)
    grad_x, grad_filters = pl.pallas_call(
        unpack_kernel,
        out_shape=(
            jax.ShapeDtypeStruct((blocks, rows, channels), jnp.bfloat16),
            jax.ShapeDtypeStruct((blocks * rows, channels), jnp.float32),
        ),
        in_specs=[vmem],
        out_specs=(vmem, vmem),
        compiler_params=params,
    )(home)
    return grad_x, grad_filters


def solution(mesh):
    placed = (P("seq", None, "chan"), P("seq", None, "chan"), P("seq", "chan"), P())
    return jax.shard_map(
        per_device,
        mesh=mesh,
        in_specs=placed,
        out_specs=(P("seq", None, "chan"), P("seq", "chan")),
        check_vma=False,
    )
```

```python
import functools

import jax
import jax.numpy as jnp
from jax import lax
from jax.experimental import pallas as pl
from jax.experimental.pallas import tpu as pltpu
from jax.sharding import PartitionSpec as P

VMEM_LIMIT = 48 * 1024 * 1024
UNROLL = 4


def permuter(size, flip):
    rows = lax.broadcasted_iota(jnp.int32, (size, size), 0)
    cols = lax.broadcasted_iota(jnp.int32, (size, size), 1)
    if flip:
        cols = size - 1 - cols
    return (rows == cols).astype(jnp.float32).astype(jnp.bfloat16)


def transposed(eye, value):
    return lax.dot_general(
        eye, value, (((1,), (1,)), ((), ())), preferred_element_type=jnp.float32
    )


def pack_kernel(x_hbm, g_hbm, h_hbm, out_ref, x_ref, g_ref, h_ref, sems):
    peers, _, blocks, part, rows = out_ref.shape
    channels = peers * part
    copies = [
        pltpu.make_async_copy(source, target, sems.at[i])
        for i, (source, target) in enumerate(
            ((x_hbm, x_ref), (g_hbm, g_ref), (h_hbm, h_ref))
        )
    ]
    for copy in copies:
        copy.start()
    for copy in copies:
        copy.wait()
    eye = permuter(channels, False)
    flip = permuter(rows, True)
    for b in range(blocks):
        flipped = jnp.dot(flip, g_ref[b], preferred_element_type=jnp.float32)
        for a, value in enumerate(
            (x_ref[b], flipped.astype(jnp.bfloat16), h_ref[b * rows : (b + 1) * rows, :])
        ):
            out_ref[:, a, b] = (
                transposed(eye, value).astype(jnp.bfloat16).reshape(peers, part, rows)
            )


def unpack_kernel(in_ref, gx_ref, gf_ref):
    peers, _, blocks, part, rows = in_ref.shape
    channels = peers * part
    eye = permuter(rows, True)
    for b in range(blocks):
        high = in_ref[:, 0, b].reshape(channels, rows)
        low = in_ref[:, 1, b].reshape(channels, rows)
        dx = in_ref[:, 2, b].reshape(channels, rows)
        gf_ref[b * rows : (b + 1) * rows, :] = transposed(eye, high) + transposed(eye, low)
        gx_ref[b] = transposed(eye, dx).astype(jnp.bfloat16)


def conv_kernel(order_ref, in_ref, out_ref, xs, seq, ub, res):
    f32, bf16 = jnp.float32, jnp.bfloat16
    peers, _, blocks, part, rows = in_ref.shape
    total = peers * blocks
    fine = 16
    coarse = rows // fine
    groups = total // coarse

    def lane(shape):
        return lax.broadcasted_iota(jnp.int32, shape, 1)

    def row(shape):
        return lax.broadcasted_iota(jnp.int32, shape, 0)

    for j in range(total):
        place = order_ref[j]
        xs[place] = in_ref[j // blocks, 0, j % blocks]
        seq[place] = in_ref[j // blocks, 1, j % blocks].astype(f32)
    seq[total] = jnp.zeros((part, rows), f32)
    chunk = lane((part, rows)) // fine
    for v in range(2):
        for g in range(groups):
            tiles = []
            for i in range(coarse):
                k = g * coarse + i
                t = xs[k] if v == 0 else in_ref[k // blocks, 2, k % blocks]
                tiles.append(t.astype(f32))
            d = 1
            while d < coarse:
                odd = (chunk // d) % 2 == 1
                for i in range(coarse):
                    if (i // d) % 2 == 0:
                        a, b = tiles[i], tiles[i + d]
                        tiles[i] = jnp.where(odd, pltpu.roll(b, fine * d, 1), a)
                        tiles[i + d] = jnp.where(odd, b, pltpu.roll(a, rows - fine * d, 1))
                d *= 2
            for e in range(coarse):
                ub[v, e, g] = tiles[e]
    upper = lane((fine, rows)) >= row((fine, rows))
    stair = lane((coarse, rows)) >= fine * row((coarse, rows))
    lanes = lane((fine, rows))
    last = row((2 * fine, rows)) == 2 * fine - 1
    def channel(c):
        def slanted(k):
            line = jnp.broadcast_to(seq[k, pl.ds(c, 1), :], (fine, rows))
            return pltpu.roll(line, 0, 1, stride=1, stride_axis=0)
        weights = []
        now = slanted(0)
        for k in range(total):
            after = slanted(k + 1) if k + 1 < total else jnp.zeros((fine, rows), f32)
            weights.append(jnp.where(upper, now, after).astype(bf16))
            now = after
        w0 = jnp.concatenate(weights[: total // 2], axis=0)
        w1 = jnp.concatenate(weights[total // 2 :], axis=0)
        near, far = [], []
        for e in range(coarse):
            for v in range(2):
                before = jnp.zeros((coarse, rows), f32)
                shifted = [before]
                for g in range(groups):
                    line = jnp.broadcast_to(ub[v, e, g, pl.ds(c, 1), :], (coarse, rows))
                    turned = pltpu.roll(line, 0, 1, stride=fine, stride_axis=0)
                    shifted.append(jnp.where(stair, turned, before))
                    before = turned
                pairs = [jnp.concatenate([shifted[g + 1], shifted[g]], axis=0).astype(bf16) for g in range(groups)]
                near.append(jnp.concatenate(pairs[:2], axis=1))
                far.append(jnp.concatenate(pairs[2:], axis=1))
        a01 = jnp.concatenate(near, axis=0)
        a23 = jnp.concatenate(far, axis=0)
        first = jnp.dot(a01, jnp.concatenate([w0, w1], axis=1), preferred_element_type=f32)
        second = jnp.dot(a23, w1, preferred_element_type=f32)
        low = first[:, :rows] + second
        high = first[:, rows:]
        for v in range(2):
            halves = []
            for half in (low, high):
                straight = half[v * fine : (v + 1) * fine]
                wrapped = jnp.zeros((fine, rows), f32)
                for e in range(1, coarse):
                    at = (2 * e + v) * fine
                    turned = pltpu.roll(half[at : at + fine], fine * e, 1)
                    straight += jnp.where(lanes >= fine * e, turned, 0.0)
                    wrapped += jnp.where(lanes >= fine * e, 0.0, turned)
                halves.append((straight, wrapped))
            straight = jnp.concatenate([h[0] for h in halves], axis=0)
            wrapped = jnp.concatenate([h[1] for h in halves], axis=0)
            wrapped = jnp.where(last, 0.0, pltpu.roll(wrapped, 2 * fine - 1, 0))
            res[c, v * total : (v + 1) * total] = straight + wrapped
    def body(i, carry):
        for u in range(UNROLL):
            channel(i * UNROLL + u)
        return carry
    lax.fori_loop(0, part // UNROLL, body, 0)
    results = res.reshape(part * 2 * total, rows)
    for j in range(total):
        place = order_ref[j]
        value = results[pl.ds(j, part, stride=2 * total), :]
        dx = results[pl.ds(total + place, part, stride=2 * total), :]
        high = value.astype(bf16)
        out_ref[j // blocks, 0, j % blocks] = high
        out_ref[j // blocks, 1, j % blocks] = (value - high.astype(f32)).astype(bf16)
        out_ref[j // blocks, 2, j % blocks] = dx.astype(bf16)


def per_device(x_groups, grad_groups, filters, group_order):
    blocks, rows, channels = x_groups.shape
    peers = lax.axis_size("seq")
    part = channels // peers
    total = peers * blocks
    vmem = pl.BlockSpec(memory_space=pltpu.VMEM)
    smem = pl.BlockSpec(memory_space=pltpu.SMEM)
    params = pltpu.CompilerParams(vmem_limit_bytes=VMEM_LIMIT)
    packed = jax.ShapeDtypeStruct((peers, 3, blocks, part, rows), jnp.bfloat16)
    send = pl.pallas_call(
        pack_kernel,
        out_shape=packed,
        in_specs=[pl.BlockSpec(memory_space=pl.ANY)] * 3,
        out_specs=vmem,
        scratch_shapes=[
            pltpu.VMEM((blocks, rows, channels), jnp.bfloat16),
            pltpu.VMEM((blocks, rows, channels), jnp.bfloat16),
            pltpu.VMEM((blocks * rows, channels), jnp.bfloat16),
            pltpu.SemaphoreType.DMA((3,)),
        ],
    )(x_groups, grad_groups, filters)
    got = lax.all_to_all(send, "seq", 0, 0, tiled=True)
    back = pl.pallas_call(
        conv_kernel,
        out_shape=packed,
        in_specs=[smem, vmem],
        out_specs=vmem,
        scratch_shapes=[
            pltpu.VMEM((total, part, rows), jnp.bfloat16),
            pltpu.VMEM((total + 1, part, rows), jnp.float32),
            pltpu.VMEM((2, rows // 16, total * 16 // rows, part, rows), jnp.float32),
            pltpu.VMEM((part, 2 * total, rows), jnp.float32),
        ],
        compiler_params=params,
    )(group_order, got)
    home = lax.all_to_all(back, "seq", 0, 0, tiled=True)
    grad_x, grad_filters = pl.pallas_call(
        unpack_kernel,
        out_shape=(
            jax.ShapeDtypeStruct((blocks, rows, channels), jnp.bfloat16),
            jax.ShapeDtypeStruct((blocks * rows, channels), jnp.float32),
        ),
        in_specs=[vmem],
        out_specs=(vmem, vmem),
        compiler_params=params,
    )(home)
    return grad_x, grad_filters


def solution(mesh):
    placed = (P("seq", None, "chan"), P("seq", None, "chan"), P("seq", "chan"), P())
    return jax.shard_map(
        per_device,
        mesh=mesh,
        in_specs=placed,
        out_specs=(P("seq", None, "chan"), P("seq", "chan")),
        check_vma=False,
    )
```

```python
import functools

import jax
import jax.numpy as jnp
from jax import lax
from jax.experimental import pallas as pl
from jax.experimental.pallas import tpu as pltpu
from jax.sharding import PartitionSpec as P

VMEM_LIMIT = 48 * 1024 * 1024
UNROLL = 4
CODE_SCALE = 2.0**30


def permuter(size, flip):
    rows = lax.broadcasted_iota(jnp.int32, (size, size), 0)
    cols = lax.broadcasted_iota(jnp.int32, (size, size), 1)
    if flip:
        cols = size - 1 - cols
    return (rows == cols).astype(jnp.float32).astype(jnp.bfloat16)


def transposed(eye, value):
    return lax.dot_general(
        eye, value, (((1,), (1,)), ((), ())), preferred_element_type=jnp.float32
    )


def pack_kernel(x_hbm, g_hbm, h_hbm, out_ref, x_ref, g_ref, h_ref, sems):
    peers, _, blocks, part, rows = out_ref.shape
    channels = peers * part
    copies = [
        pltpu.make_async_copy(source, target, sems.at[i])
        for i, (source, target) in enumerate(
            ((x_hbm, x_ref), (g_hbm, g_ref), (h_hbm, h_ref))
        )
    ]
    for copy in copies:
        copy.start()
    for copy in copies:
        copy.wait()
    eye = permuter(channels, False)
    flip = permuter(rows, True)
    for b in range(blocks):
        flipped = jnp.dot(flip, g_ref[b], preferred_element_type=jnp.float32)
        for a, value in enumerate(
            (x_ref[b], flipped.astype(jnp.bfloat16), h_ref[b * rows : (b + 1) * rows, :])
        ):
            out_ref[:, a, b] = (
                transposed(eye, value).astype(jnp.bfloat16).reshape(peers, part, rows)
            )


def unpack_kernel(in_ref, gx_ref, gf_ref):
    peers, _, blocks, part, rows = in_ref.shape
    channels = peers * part
    eye = permuter(rows, True)
    for b in range(blocks):
        cube = transposed(eye, in_ref[:, 0, b].reshape(channels, rows))
        dx = in_ref[:, 1, b].reshape(channels, rows)
        size = jnp.exp2(jnp.log2(jnp.abs(cube)) * (1.0 / 3.0)) * (1.0 / CODE_SCALE)
        size = jnp.where(cube == 0.0, 0.0, size)
        gf_ref[b * rows : (b + 1) * rows, :] = jnp.where(cube < 0.0, -size, size)
        gx_ref[b] = transposed(eye, dx).astype(jnp.bfloat16)


def conv_kernel(order_ref, in_ref, out_ref, xs, seq, ub, res):
    f32, bf16 = jnp.float32, jnp.bfloat16
    peers, _, blocks, part, rows = in_ref.shape
    total = peers * blocks
    fine = 16
    coarse = rows // fine
    groups = total // coarse

    def lane(shape):
        return lax.broadcasted_iota(jnp.int32, shape, 1)

    def row(shape):
        return lax.broadcasted_iota(jnp.int32, shape, 0)

    for j in range(total):
        place = order_ref[j]
        xs[place] = in_ref[j // blocks, 0, j % blocks]
        seq[place] = in_ref[j // blocks, 1, j % blocks].astype(f32)
    seq[total] = jnp.zeros((part, rows), f32)
    chunk = lane((part, rows)) // fine
    for v in range(2):
        for g in range(groups):
            tiles = []
            for i in range(coarse):
                k = g * coarse + i
                t = xs[k] if v == 0 else in_ref[k // blocks, 2, k % blocks]
                tiles.append(t.astype(f32))
            d = 1
            while d < coarse:
                odd = (chunk // d) % 2 == 1
                for i in range(coarse):
                    if (i // d) % 2 == 0:
                        a, b = tiles[i], tiles[i + d]
                        tiles[i] = jnp.where(odd, pltpu.roll(b, fine * d, 1), a)
                        tiles[i + d] = jnp.where(odd, b, pltpu.roll(a, rows - fine * d, 1))
                d *= 2
            for e in range(coarse):
                ub[v, e, g] = tiles[e]
    upper = lane((fine, rows)) >= row((fine, rows))
    stair = lane((coarse, rows)) >= fine * row((coarse, rows))
    lanes = lane((fine, rows))
    last = row((2 * fine, rows)) == 2 * fine - 1
    def channel(c):
        def slanted(k):
            line = jnp.broadcast_to(seq[k, pl.ds(c, 1), :], (fine, rows))
            return pltpu.roll(line, 0, 1, stride=1, stride_axis=0)
        weights = []
        now = slanted(0)
        for k in range(total):
            after = slanted(k + 1) if k + 1 < total else jnp.zeros((fine, rows), f32)
            weights.append(jnp.where(upper, now, after).astype(bf16))
            now = after
        w0 = jnp.concatenate(weights[: total // 2], axis=0)
        w1 = jnp.concatenate(weights[total // 2 :], axis=0)
        near, far = [], []
        for e in range(coarse):
            for v in range(2):
                before = jnp.zeros((coarse, rows), f32)
                shifted = [before]
                for g in range(groups):
                    line = jnp.broadcast_to(ub[v, e, g, pl.ds(c, 1), :], (coarse, rows))
                    turned = pltpu.roll(line, 0, 1, stride=fine, stride_axis=0)
                    shifted.append(jnp.where(stair, turned, before))
                    before = turned
                pairs = [jnp.concatenate([shifted[g + 1], shifted[g]], axis=0).astype(bf16) for g in range(groups)]
                near.append(jnp.concatenate(pairs[:2], axis=1))
                far.append(jnp.concatenate(pairs[2:], axis=1))
        a01 = jnp.concatenate(near, axis=0)
        a23 = jnp.concatenate(far, axis=0)
        first = jnp.dot(a01, jnp.concatenate([w0, w1], axis=1), preferred_element_type=f32)
        second = jnp.dot(a23, w1, preferred_element_type=f32)
        low = first[:, :rows] + second
        high = first[:, rows:]
        for v in range(2):
            halves = []
            for half in (low, high):
                straight = half[v * fine : (v + 1) * fine]
                wrapped = jnp.zeros((fine, rows), f32)
                for e in range(1, coarse):
                    at = (2 * e + v) * fine
                    turned = pltpu.roll(half[at : at + fine], fine * e, 1)
                    straight += jnp.where(lanes >= fine * e, turned, 0.0)
                    wrapped += jnp.where(lanes >= fine * e, 0.0, turned)
                halves.append((straight, wrapped))
            straight = jnp.concatenate([h[0] for h in halves], axis=0)
            wrapped = jnp.concatenate([h[1] for h in halves], axis=0)
            wrapped = jnp.where(last, 0.0, pltpu.roll(wrapped, 2 * fine - 1, 0))
            res[c, v * total : (v + 1) * total] = straight + wrapped
    def body(i, carry):
        for u in range(UNROLL):
            channel(i * UNROLL + u)
        return carry
    lax.fori_loop(0, part // UNROLL, body, 0)
    results = res.reshape(part * 2 * total, rows)
    for j in range(total):
        place = order_ref[j]
        value = results[pl.ds(j, part, stride=2 * total), :]
        dx = results[pl.ds(total + place, part, stride=2 * total), :]
        value = value * CODE_SCALE
        out_ref[j // blocks, 0, j % blocks] = (value * value * value).astype(bf16)
        out_ref[j // blocks, 1, j % blocks] = dx.astype(bf16)


def per_device(x_groups, grad_groups, filters, group_order):
    blocks, rows, channels = x_groups.shape
    peers = lax.axis_size("seq")
    part = channels // peers
    total = peers * blocks
    vmem = pl.BlockSpec(memory_space=pltpu.VMEM)
    smem = pl.BlockSpec(memory_space=pltpu.SMEM)
    params = pltpu.CompilerParams(vmem_limit_bytes=VMEM_LIMIT)
    packed = jax.ShapeDtypeStruct((peers, 3, blocks, part, rows), jnp.bfloat16)
    coded = jax.ShapeDtypeStruct((peers, 2, blocks, part, rows), jnp.bfloat16)
    send = pl.pallas_call(
        pack_kernel,
        out_shape=packed,
        in_specs=[pl.BlockSpec(memory_space=pl.ANY)] * 3,
        out_specs=vmem,
        scratch_shapes=[
            pltpu.VMEM((blocks, rows, channels), jnp.bfloat16),
            pltpu.VMEM((blocks, rows, channels), jnp.bfloat16),
            pltpu.VMEM((blocks * rows, channels), jnp.bfloat16),
            pltpu.SemaphoreType.DMA((3,)),
        ],
    )(x_groups, grad_groups, filters)
    got = lax.all_to_all(send, "seq", 0, 0, tiled=True)
    back = pl.pallas_call(
        conv_kernel,
        out_shape=coded,
        in_specs=[smem, vmem],
        out_specs=vmem,
        scratch_shapes=[
            pltpu.VMEM((total, part, rows), jnp.bfloat16),
            pltpu.VMEM((total + 1, part, rows), jnp.float32),
            pltpu.VMEM((2, rows // 16, total * 16 // rows, part, rows), jnp.float32),
            pltpu.VMEM((part, 2 * total, rows), jnp.float32),
        ],
        compiler_params=params,
    )(group_order, got)
    home = lax.all_to_all(back, "seq", 0, 0, tiled=True)
    grad_x, grad_filters = pl.pallas_call(
        unpack_kernel,
        out_shape=(
            jax.ShapeDtypeStruct((blocks, rows, channels), jnp.bfloat16),
            jax.ShapeDtypeStruct((blocks * rows, channels), jnp.float32),
        ),
        in_specs=[vmem],
        out_specs=(vmem, vmem),
        compiler_params=params,
    )(home)
    return grad_x, grad_filters


def solution(mesh):
    placed = (P("seq", None, "chan"), P("seq", None, "chan"), P("seq", "chan"), P())
    return jax.shard_map(
        per_device,
        mesh=mesh,
        in_specs=placed,
        out_specs=(P("seq", None, "chan"), P("seq", "chan")),
        check_vma=False,
    )
```

```python
import functools

import jax
import jax.numpy as jnp
from jax import lax
from jax.experimental import pallas as pl
from jax.experimental.pallas import tpu as pltpu
from jax.sharding import PartitionSpec as P

VMEM_LIMIT = 48 * 1024 * 1024
UNROLL = 8
CODE_SCALE = 2.0**30


def permuter(size, flip):
    rows = lax.broadcasted_iota(jnp.int32, (size, size), 0)
    cols = lax.broadcasted_iota(jnp.int32, (size, size), 1)
    if flip:
        cols = size - 1 - cols
    return (rows == cols).astype(jnp.float32).astype(jnp.bfloat16)


def transposed(eye, value):
    return lax.dot_general(
        eye, value, (((1,), (1,)), ((), ())), preferred_element_type=jnp.float32
    )


def pack_kernel(x_hbm, g_hbm, h_hbm, out_ref, x_ref, g_ref, h_ref, sems):
    peers, _, blocks, part, rows = out_ref.shape
    channels = peers * part
    copies = [
        pltpu.make_async_copy(source, target, sems.at[i])
        for i, (source, target) in enumerate(
            ((g_hbm, g_ref), (x_hbm, x_ref), (h_hbm, h_ref))
        )
    ]
    for copy in copies:
        copy.start()
    flip = permuter(rows, True)

    def put(a, b, value):
        out_ref[:, a, b] = value.astype(jnp.bfloat16).reshape(peers, part, rows)

    copies[0].wait()
    for b in range(blocks):
        put(1, b, jnp.dot(g_ref[b].T, flip, preferred_element_type=jnp.float32))
    copies[1].wait()
    for b in range(blocks):
        put(0, b, x_ref[b].T)
    copies[2].wait()
    for b in range(blocks):
        put(2, b, h_ref[b * rows : (b + 1) * rows, :].T)


def unpack_kernel(in_ref, gx_ref, gf_ref):
    peers, _, blocks, part, rows = in_ref.shape
    channels = peers * part
    eye = permuter(rows, True)
    for b in range(blocks):
        cube = transposed(eye, in_ref[:, 0, b].reshape(channels, rows))
        dx = in_ref[:, 1, b].reshape(channels, rows)
        size = jnp.exp2(jnp.log2(jnp.abs(cube)) * (1.0 / 3.0)) * (1.0 / CODE_SCALE)
        size = jnp.where(cube == 0.0, 0.0, size)
        gf_ref[b * rows : (b + 1) * rows, :] = jnp.where(cube < 0.0, -size, size)
        gx_ref[b] = transposed(eye, dx).astype(jnp.bfloat16)


def conv_kernel(order_ref, in_ref, out_ref, xs, seq, ub, res, wbuf, abuf):
    f32, bf16 = jnp.float32, jnp.bfloat16
    peers, _, blocks, part, rows = in_ref.shape
    total = peers * blocks
    fine = 16
    coarse = rows // fine
    groups = total // coarse

    def lane(shape):
        return lax.broadcasted_iota(jnp.int32, shape, 1)

    def row(shape):
        return lax.broadcasted_iota(jnp.int32, shape, 0)

    for j in range(total):
        place = order_ref[j]
        xs[place] = in_ref[j // blocks, 0, j % blocks]
        seq[place] = in_ref[j // blocks, 1, j % blocks].astype(f32)
    chunk = lane((part, rows)) // fine
    for v in range(2):
        for g in range(groups):
            tiles = []
            for i in range(coarse):
                k = g * coarse + i
                t = xs[k] if v == 0 else in_ref[k // blocks, 2, k % blocks]
                tiles.append(t.astype(f32))
            d = 1
            while d < coarse:
                odd = (chunk // d) % 2 == 1
                for i in range(coarse):
                    if (i // d) % 2 == 0:
                        a, b = tiles[i], tiles[i + d]
                        tiles[i] = jnp.where(odd, pltpu.roll(b, fine * d, 1), a)
                        tiles[i + d] = jnp.where(odd, b, pltpu.roll(a, rows - fine * d, 1))
                d *= 2
            for e in range(coarse):
                ub[v, e, g] = tiles[e]
    upper = lane((fine, rows)) >= row((fine, rows))
    stair = lane((coarse, rows)) >= fine * row((coarse, rows))
    lanes = lane((fine, rows))
    last = row((2 * fine, rows)) == 2 * fine - 1
    def prepare(c, slot):
        def slanted(k):
            line = jnp.broadcast_to(seq[k, pl.ds(c, 1), :], (fine, rows)).astype(bf16)
            return pltpu.roll(line, 0, 1, stride=1, stride_axis=0)
        now = slanted(0)
        for k in range(total):
            after = slanted(k + 1) if k + 1 < total else jnp.zeros((fine, rows), bf16)
            wbuf[slot, k * fine : (k + 1) * fine, :] = jnp.where(upper, now, after)
            now = after
        for e in range(coarse):
            for v in range(2):
                before = jnp.zeros((coarse, rows), f32)
                shifted = [before]
                for g in range(groups):
                    line = jnp.broadcast_to(ub[v, e, g, pl.ds(c, 1), :], (coarse, rows))
                    turned = pltpu.roll(line, 0, 1, stride=fine, stride_axis=0)
                    shifted.append(jnp.where(stair, turned, before))
                    before = turned
                at = (2 * e + v) * fine
                for g in range(groups):
                    abuf[slot, at : at + fine, g * rows : (g + 1) * rows] = jnp.concatenate([shifted[g + 1], shifted[g]], axis=0).astype(bf16)
    def finish(c, slot):
        half_k = total // 2 * fine
        w1 = wbuf[slot, half_k:, :]
        first = jnp.dot(
            abuf[slot, :, : 2 * rows],
            jnp.concatenate([wbuf[slot, :half_k, :], w1], axis=1),
            preferred_element_type=f32,
        )
        second = jnp.dot(abuf[slot, :, 2 * rows :], w1, preferred_element_type=f32)
        low = first[:, :rows] + second
        high = first[:, rows:]
        for v in range(2):
            halves = []
            for half in (low, high):
                straight = half[v * fine : (v + 1) * fine]
                wrapped = jnp.zeros((fine, rows), f32)
                for e in range(1, coarse):
                    at = (2 * e + v) * fine
                    turned = pltpu.roll(half[at : at + fine], fine * e, 1)
                    keep = jnp.where(lanes >= fine * e, turned, 0.0)
                    straight += keep
                    wrapped += turned - keep
                halves.append((straight, wrapped))
            straight = jnp.concatenate([h[0] for h in halves], axis=0)
            wrapped = jnp.concatenate([h[1] for h in halves], axis=0)
            wrapped = jnp.where(last, 0.0, pltpu.roll(wrapped, 2 * fine - 1, 0))
            res[c, v * total : (v + 1) * total] = straight + wrapped

    def body(i, carry):
        for u in range(UNROLL):
            prepare(i * UNROLL + u, u)
        for u in range(UNROLL):
            finish(i * UNROLL + u, u)
        return carry

    lax.fori_loop(0, part // UNROLL, body, 0)
    results = res.reshape(part * 2 * total, rows)
    for j in range(total):
        place = order_ref[j]
        value = results[pl.ds(j, part, stride=2 * total), :]
        dx = results[pl.ds(total + place, part, stride=2 * total), :]
        value = value * CODE_SCALE
        out_ref[j // blocks, 0, j % blocks] = (value * value * value).astype(bf16)
        out_ref[j // blocks, 1, j % blocks] = dx.astype(bf16)


def per_device(x_groups, grad_groups, filters, group_order):
    blocks, rows, channels = x_groups.shape
    peers = lax.axis_size("seq")
    part = channels // peers
    total = peers * blocks
    vmem = pl.BlockSpec(memory_space=pltpu.VMEM)
    smem = pl.BlockSpec(memory_space=pltpu.SMEM)
    params = pltpu.CompilerParams(vmem_limit_bytes=VMEM_LIMIT)
    packed = jax.ShapeDtypeStruct((peers, 3, blocks, part, rows), jnp.bfloat16)
    coded = jax.ShapeDtypeStruct((peers, 2, blocks, part, rows), jnp.bfloat16)
    send = pl.pallas_call(
        pack_kernel,
        out_shape=packed,
        in_specs=[pl.BlockSpec(memory_space=pl.ANY)] * 3,
        out_specs=vmem,
        scratch_shapes=[
            pltpu.VMEM((blocks, rows, channels), jnp.bfloat16),
            pltpu.VMEM((blocks, rows, channels), jnp.bfloat16),
            pltpu.VMEM((blocks * rows, channels), jnp.bfloat16),
            pltpu.SemaphoreType.DMA((3,)),
        ],
    )(x_groups, grad_groups, filters)
    got = lax.all_to_all(send, "seq", 0, 0, tiled=True)
    back = pl.pallas_call(
        conv_kernel,
        out_shape=coded,
        in_specs=[smem, vmem],
        out_specs=vmem,
        scratch_shapes=[
            pltpu.VMEM((total, part, rows), jnp.bfloat16),
            pltpu.VMEM((total + 1, part, rows), jnp.float32),
            pltpu.VMEM((2, rows // 16, total * 16 // rows, part, rows), jnp.float32),
            pltpu.VMEM((part, 2 * total, rows), jnp.float32),
            pltpu.VMEM((UNROLL, 16 * total, rows), jnp.bfloat16),
            pltpu.VMEM((UNROLL, 2 * rows, 16 * total), jnp.bfloat16),
        ],
        compiler_params=params,
    )(group_order, got)
    home = lax.all_to_all(back, "seq", 0, 0, tiled=True)
    grad_x, grad_filters = pl.pallas_call(
        unpack_kernel,
        out_shape=(
            jax.ShapeDtypeStruct((blocks, rows, channels), jnp.bfloat16),
            jax.ShapeDtypeStruct((blocks * rows, channels), jnp.float32),
        ),
        in_specs=[vmem],
        out_specs=(vmem, vmem),
        compiler_params=params,
    )(home)
    return grad_x, grad_filters


def solution(mesh):
    placed = (P("seq", None, "chan"), P("seq", None, "chan"), P("seq", "chan"), P())
    return jax.shard_map(
        per_device,
        mesh=mesh,
        in_specs=placed,
        out_specs=(P("seq", None, "chan"), P("seq", "chan")),
        check_vma=False,
    )
```

```python
import functools

import jax
import jax.numpy as jnp
from jax import lax
from jax.experimental import pallas as pl
from jax.experimental.pallas import tpu as pltpu
from jax.sharding import PartitionSpec as P

VMEM_LIMIT = 48 * 1024 * 1024
UNROLL = 16
CODE_SCALE = 2.0**30


def permuter(size, flip):
    rows = lax.broadcasted_iota(jnp.int32, (size, size), 0)
    cols = lax.broadcasted_iota(jnp.int32, (size, size), 1)
    if flip:
        cols = size - 1 - cols
    return (rows == cols).astype(jnp.float32).astype(jnp.bfloat16)


def transposed(eye, value):
    return lax.dot_general(
        eye, value, (((1,), (1,)), ((), ())), preferred_element_type=jnp.float32
    )


def pack_kernel(x_hbm, g_hbm, h_hbm, out_ref, x_ref, g_ref, h_ref, sems):
    peers, _, blocks, part, rows = out_ref.shape
    channels = peers * part
    copies = [
        pltpu.make_async_copy(source, target, sems.at[i])
        for i, (source, target) in enumerate(
            ((g_hbm, g_ref), (x_hbm, x_ref), (h_hbm, h_ref))
        )
    ]
    for copy in copies:
        copy.start()
    flip = permuter(rows, True)

    def put(a, b, value):
        out_ref[:, a, b] = value.astype(jnp.bfloat16).reshape(peers, part, rows)

    copies[0].wait()
    for b in range(blocks):
        put(1, b, jnp.dot(g_ref[b].T, flip, preferred_element_type=jnp.float32))
    copies[1].wait()
    for b in range(blocks):
        put(0, b, x_ref[b].T)
    copies[2].wait()
    for b in range(blocks):
        put(2, b, h_ref[b * rows : (b + 1) * rows, :].T)


def unpack_kernel(in_ref, gx_ref, gf_ref):
    peers, _, blocks, part, rows = in_ref.shape
    channels = peers * part
    eye = permuter(rows, True)
    for b in range(blocks):
        cube = transposed(eye, in_ref[:, 0, b].reshape(channels, rows))
        dx = in_ref[:, 1, b].reshape(channels, rows)
        size = jnp.exp2(jnp.log2(jnp.abs(cube)) * (1.0 / 3.0)) * (1.0 / CODE_SCALE)
        size = jnp.where(cube == 0.0, 0.0, size)
        gf_ref[b * rows : (b + 1) * rows, :] = jnp.where(cube < 0.0, -size, size)
        gx_ref[b] = transposed(eye, dx).astype(jnp.bfloat16)


def conv_kernel(order_any, in_ref, out_ref, xs, seq, ub, res, wbuf, abuf, order_ref, order_sem):
    f32, bf16 = jnp.float32, jnp.bfloat16
    peers, _, blocks, part, rows = in_ref.shape
    total = peers * blocks
    order_copy = pltpu.make_async_copy(order_any, order_ref, order_sem)
    order_copy.start()
    fine = 16
    coarse = rows // fine
    groups = total // coarse

    def lane(shape):
        return lax.broadcasted_iota(jnp.int32, shape, 1)

    def row(shape):
        return lax.broadcasted_iota(jnp.int32, shape, 0)

    chunk = lane((part, rows)) // fine
    def regroup(v):
        for g in range(groups):
            tiles = []
            for i in range(coarse):
                k = g * coarse + i
                t = xs[k] if v == 0 else in_ref[k // blocks, 2, k % blocks]
                tiles.append(t.astype(f32))
            d = 1
            while d < coarse:
                odd = (chunk // d) % 2 == 1
                for i in range(coarse):
                    if (i // d) % 2 == 0:
                        a, b = tiles[i], tiles[i + d]
                        tiles[i] = jnp.where(odd, pltpu.roll(b, fine * d, 1), a)
                        tiles[i + d] = jnp.where(odd, b, pltpu.roll(a, rows - fine * d, 1))
                d *= 2
            for e in range(coarse):
                ub[v, e, g] = tiles[e]
    upper = lane((fine, rows)) >= row((fine, rows))
    stair = lane((coarse, rows)) >= fine * row((coarse, rows))
    lanes = lane((fine, rows))
    last = row((2 * fine, rows)) == 2 * fine - 1
    def prepare_right(c, slot):
        def slanted(k):
            line = jnp.broadcast_to(seq[k, pl.ds(c, 1), :], (fine, rows)).astype(bf16)
            return pltpu.roll(line, 0, 1, stride=1, stride_axis=0)
        now = slanted(0)
        for k in range(total):
            after = slanted(k + 1) if k + 1 < total else jnp.zeros((fine, rows), bf16)
            wbuf[slot, k * fine : (k + 1) * fine, :] = jnp.where(upper, now, after)
            now = after
    def prepare_left(c, slot, v):
        for e in range(coarse):
            before = jnp.zeros((coarse, rows), f32)
            shifted = [before]
            for g in range(groups):
                line = jnp.broadcast_to(ub[v, e, g, pl.ds(c, 1), :], (coarse, rows))
                turned = pltpu.roll(line, 0, 1, stride=fine, stride_axis=0)
                shifted.append(jnp.where(stair, turned, before))
                before = turned
            at = (2 * e + v) * fine
            for g in range(groups):
                abuf[slot, at : at + fine, g * rows : (g + 1) * rows] = jnp.concatenate([shifted[g + 1], shifted[g]], axis=0).astype(bf16)
    def finish(c, slot):
        half_k = total // 2 * fine
        w1 = wbuf[slot, half_k:, :]
        first = jnp.dot(
            abuf[slot, :, : 2 * rows],
            jnp.concatenate([wbuf[slot, :half_k, :], w1], axis=1),
            preferred_element_type=f32,
        )
        second = jnp.dot(abuf[slot, :, 2 * rows :], w1, preferred_element_type=f32)
        low = first[:, :rows] + second
        high = first[:, rows:]
        for v in range(2):
            halves = []
            for half in (low, high):
                straight = half[v * fine : (v + 1) * fine]
                wrapped = jnp.zeros((fine, rows), f32)
                for e in range(1, coarse):
                    at = (2 * e + v) * fine
                    turned = pltpu.roll(half[at : at + fine], fine * e, 1)
                    keep = jnp.where(lanes >= fine * e, turned, 0.0)
                    straight += keep
                    wrapped += turned - keep
                halves.append((straight, wrapped))
            straight = jnp.concatenate([h[0] for h in halves], axis=0)
            wrapped = jnp.concatenate([h[1] for h in halves], axis=0)
            wrapped = jnp.where(last, 0.0, pltpu.roll(wrapped, 2 * fine - 1, 0))
            res[c, v * total : (v + 1) * total] = straight + wrapped

    regroup(1)
    for u in range(UNROLL):
        prepare_left(u, u, 1)
    order_copy.wait()
    for j in range(total):
        place = order_ref[j]
        xs[place] = in_ref[j // blocks, 0, j % blocks]
        seq[place] = in_ref[j // blocks, 1, j % blocks].astype(f32)
    regroup(0)
    for first in range(0, part, UNROLL):
        for u in range(UNROLL):
            prepare_right(first + u, u)
            prepare_left(first + u, u, 0)
            if first:
                prepare_left(first + u, u, 1)
        for u in range(UNROLL):
            finish(first + u, u)
    results = res.reshape(part * 2 * total, rows)
    for j in range(total):
        place = order_ref[j]
        value = results[pl.ds(j, part, stride=2 * total), :]
        dx = results[pl.ds(total + place, part, stride=2 * total), :]
        value = value * CODE_SCALE
        out_ref[j // blocks, 0, j % blocks] = (value * value * value).astype(bf16)
        out_ref[j // blocks, 1, j % blocks] = dx.astype(bf16)


def per_device(x_groups, grad_groups, filters, group_order):
    blocks, rows, channels = x_groups.shape
    peers = lax.axis_size("seq")
    part = channels // peers
    total = peers * blocks
    vmem = pl.BlockSpec(memory_space=pltpu.VMEM)
    params = pltpu.CompilerParams(vmem_limit_bytes=VMEM_LIMIT)
    packed = jax.ShapeDtypeStruct((peers, 3, blocks, part, rows), jnp.bfloat16)
    coded = jax.ShapeDtypeStruct((peers, 2, blocks, part, rows), jnp.bfloat16)
    send = pl.pallas_call(
        pack_kernel,
        out_shape=packed,
        in_specs=[pl.BlockSpec(memory_space=pl.ANY)] * 3,
        out_specs=vmem,
        scratch_shapes=[
            pltpu.VMEM((blocks, rows, channels), jnp.bfloat16),
            pltpu.VMEM((blocks, rows, channels), jnp.bfloat16),
            pltpu.VMEM((blocks * rows, channels), jnp.bfloat16),
            pltpu.SemaphoreType.DMA((3,)),
        ],
    )(x_groups, grad_groups, filters)
    got = lax.all_to_all(send, "seq", 0, 0, tiled=True)
    back = pl.pallas_call(
        conv_kernel,
        out_shape=coded,
        in_specs=[pl.BlockSpec(memory_space=pl.ANY), vmem],
        out_specs=vmem,
        scratch_shapes=[
            pltpu.VMEM((total, part, rows), jnp.bfloat16),
            pltpu.VMEM((total + 1, part, rows), jnp.float32),
            pltpu.VMEM((2, rows // 16, total * 16 // rows, part, rows), jnp.float32),
            pltpu.VMEM((part, 2 * total, rows), jnp.float32),
            pltpu.VMEM((UNROLL, 16 * total, rows), jnp.bfloat16),
            pltpu.VMEM((UNROLL, 2 * rows, 16 * total), jnp.bfloat16),
            pltpu.SMEM((total,), jnp.int32),
            pltpu.SemaphoreType.DMA,
        ],
        compiler_params=params,
    )(group_order, got)
    home = lax.all_to_all(back, "seq", 0, 0, tiled=True)
    grad_x, grad_filters = pl.pallas_call(
        unpack_kernel,
        out_shape=(
            jax.ShapeDtypeStruct((blocks, rows, channels), jnp.bfloat16),
            jax.ShapeDtypeStruct((blocks * rows, channels), jnp.float32),
        ),
        in_specs=[vmem],
        out_specs=(vmem, vmem),
        compiler_params=params,
    )(home)
    return grad_x, grad_filters


def solution(mesh):
    placed = (P("seq", None, "chan"), P("seq", None, "chan"), P("seq", "chan"), P())
    return jax.shard_map(
        per_device,
        mesh=mesh,
        in_specs=placed,
        out_specs=(P("seq", None, "chan"), P("seq", "chan")),
        check_vma=False,
    )
```

```python
import functools

import jax
import jax.numpy as jnp
from jax import lax
from jax.experimental import pallas as pl
from jax.experimental.pallas import tpu as pltpu
from jax.sharding import PartitionSpec as P

VMEM_LIMIT = 48 * 1024 * 1024
UNROLL = 16
CODE_SCALE = 2.0**30


def permuter(size, flip):
    rows = lax.broadcasted_iota(jnp.int32, (size, size), 0)
    cols = lax.broadcasted_iota(jnp.int32, (size, size), 1)
    if flip:
        cols = size - 1 - cols
    return (rows == cols).astype(jnp.float32).astype(jnp.bfloat16)


def transposed(eye, value):
    return lax.dot_general(
        eye, value, (((1,), (1,)), ((), ())), preferred_element_type=jnp.float32
    )


def pack_kernel(x_hbm, g_hbm, h_hbm, out_ref, x_ref, g_ref, h_ref, sems):
    peers, _, blocks, part, rows = out_ref.shape
    channels = peers * part
    copies = [
        pltpu.make_async_copy(source, target, sems.at[i])
        for i, (source, target) in enumerate(
            ((g_hbm, g_ref), (x_hbm, x_ref), (h_hbm, h_ref))
        )
    ]
    for copy in copies:
        copy.start()

    def put(a, b, value):
        out_ref[:, a, b] = value.astype(jnp.bfloat16).reshape(peers, part, rows)

    copies[0].wait()
    for b in range(blocks):
        put(1, b, g_ref[b].T)
    copies[1].wait()
    for b in range(blocks):
        put(0, b, x_ref[b].T)
    copies[2].wait()
    for b in range(blocks):
        put(2, b, h_ref[b * rows : (b + 1) * rows, :].T)


def unpack_kernel(in_ref, gx_ref, gf_ref):
    peers, _, blocks, part, rows = in_ref.shape
    channels = peers * part
    eye = permuter(rows, True)
    for b in range(blocks):
        cube = transposed(eye, in_ref[:, 0, b].reshape(channels, rows))
        dx = in_ref[:, 1, b].reshape(channels, rows)
        size = jnp.exp2(jnp.log2(jnp.abs(cube)) * (1.0 / 3.0)) * (1.0 / CODE_SCALE)
        size = jnp.where(cube == 0.0, 0.0, size)
        gf_ref[b * rows : (b + 1) * rows, :] = jnp.where(cube < 0.0, -size, size)
        gx_ref[b] = transposed(eye, dx).astype(jnp.bfloat16)


def conv_kernel(order_any, in_ref, out_ref, xs, seq, ub, res, wbuf, abuf, order_ref, order_sem):
    f32, bf16 = jnp.float32, jnp.bfloat16
    peers, _, blocks, part, rows = in_ref.shape
    total = peers * blocks
    order_copy = pltpu.make_async_copy(order_any, order_ref, order_sem)
    order_copy.start()
    fine = 16
    coarse = rows // fine
    groups = total // coarse

    def lane(shape):
        return lax.broadcasted_iota(jnp.int32, shape, 1)

    def row(shape):
        return lax.broadcasted_iota(jnp.int32, shape, 0)

    chunk = lane((part, rows)) // fine
    def regroup(v):
        for g in range(groups):
            tiles = []
            for i in range(coarse):
                k = g * coarse + i
                t = xs[k] if v == 0 else in_ref[k // blocks, 2, k % blocks]
                tiles.append(t.astype(f32))
            d = 1
            while d < coarse:
                odd = (chunk // d) % 2 == 1
                for i in range(coarse):
                    if (i // d) % 2 == 0:
                        a, b = tiles[i], tiles[i + d]
                        tiles[i] = jnp.where(odd, pltpu.roll(b, fine * d, 1), a)
                        tiles[i + d] = jnp.where(odd, b, pltpu.roll(a, rows - fine * d, 1))
                d *= 2
            for e in range(coarse):
                ub[v, e, g] = tiles[e]
    upper = lane((fine, rows)) >= row((fine, rows))
    stair = lane((coarse, rows)) >= fine * row((coarse, rows))
    lanes = lane((fine, rows))
    last = row((2 * fine, rows)) == 2 * fine - 1
    def prepare_right(c, slot):
        def slanted(k):
            line = jnp.broadcast_to(seq[k, pl.ds(c, 1), :], (fine, rows)).astype(bf16)
            return pltpu.roll(line, 0, 1, stride=1, stride_axis=0)
        now = slanted(0)
        for k in range(total):
            after = slanted(k + 1) if k + 1 < total else jnp.zeros((fine, rows), bf16)
            wbuf[slot, k * fine : (k + 1) * fine, :] = jnp.where(upper, now, after)
            now = after
    def prepare_left(c, slot, v):
        for e in range(coarse):
            before = jnp.zeros((coarse, rows), f32)
            shifted = [before]
            for g in range(groups):
                line = jnp.broadcast_to(ub[v, e, g, pl.ds(c, 1), :], (coarse, rows))
                turned = pltpu.roll(line, 0, 1, stride=fine, stride_axis=0)
                shifted.append(jnp.where(stair, turned, before))
                before = turned
            at = (2 * e + v) * fine
            for g in range(groups):
                abuf[slot, at : at + fine, g * rows : (g + 1) * rows] = jnp.concatenate([shifted[g + 1], shifted[g]], axis=0).astype(bf16)
    def finish(c, slot):
        half_k = total // 2 * fine
        w1 = wbuf[slot, half_k:, :]
        first = jnp.dot(
            abuf[slot, :, : 2 * rows],
            jnp.concatenate([wbuf[slot, :half_k, :], w1], axis=1),
            preferred_element_type=f32,
        )
        second = jnp.dot(abuf[slot, :, 2 * rows :], w1, preferred_element_type=f32)
        low = first[:, :rows] + second
        high = first[:, rows:]
        for v in range(2):
            halves = []
            for half in (low, high):
                straight = half[v * fine : (v + 1) * fine]
                wrapped = jnp.zeros((fine, rows), f32)
                for e in range(1, coarse):
                    at = (2 * e + v) * fine
                    turned = pltpu.roll(half[at : at + fine], fine * e, 1)
                    keep = jnp.where(lanes >= fine * e, turned, 0.0)
                    straight += keep
                    wrapped += turned - keep
                halves.append((straight, wrapped))
            straight = jnp.concatenate([h[0] for h in halves], axis=0)
            wrapped = jnp.concatenate([h[1] for h in halves], axis=0)
            wrapped = jnp.where(last, 0.0, pltpu.roll(wrapped, 2 * fine - 1, 0))
            res[c, v * total : (v + 1) * total] = straight + wrapped

    regroup(1)
    for u in range(UNROLL):
        prepare_left(u, u, 1)
    flip = permuter(rows, True)
    grads = in_ref[:, 1].reshape(total * part, rows)
    flipped = jnp.dot(grads, flip, preferred_element_type=f32)
    order_copy.wait()
    for j in range(total):
        place = order_ref[j]
        xs[place] = in_ref[j // blocks, 0, j % blocks]
        seq[place] = flipped[j * part : (j + 1) * part]
    regroup(0)
    for first in range(0, part, UNROLL):
        for u in range(UNROLL):
            prepare_right(first + u, u)
            prepare_left(first + u, u, 0)
            if first:
                prepare_left(first + u, u, 1)
        for u in range(UNROLL):
            finish(first + u, u)
    results = res.reshape(part * 2 * total, rows)
    for j in range(total):
        place = order_ref[j]
        value = results[pl.ds(j, part, stride=2 * total), :]
        dx = results[pl.ds(total + place, part, stride=2 * total), :]
        value = value * CODE_SCALE
        out_ref[j // blocks, 0, j % blocks] = (value * value * value).astype(bf16)
        out_ref[j // blocks, 1, j % blocks] = dx.astype(bf16)


def per_device(x_groups, grad_groups, filters, group_order):
    blocks, rows, channels = x_groups.shape
    peers = lax.axis_size("seq")
    part = channels // peers
    total = peers * blocks
    vmem = pl.BlockSpec(memory_space=pltpu.VMEM)
    params = pltpu.CompilerParams(vmem_limit_bytes=VMEM_LIMIT)
    packed = jax.ShapeDtypeStruct((peers, 3, blocks, part, rows), jnp.bfloat16)
    coded = jax.ShapeDtypeStruct((peers, 2, blocks, part, rows), jnp.bfloat16)
    send = pl.pallas_call(
        pack_kernel,
        out_shape=packed,
        in_specs=[pl.BlockSpec(memory_space=pl.ANY)] * 3,
        out_specs=vmem,
        scratch_shapes=[
            pltpu.VMEM((blocks, rows, channels), jnp.bfloat16),
            pltpu.VMEM((blocks, rows, channels), jnp.bfloat16),
            pltpu.VMEM((blocks * rows, channels), jnp.bfloat16),
            pltpu.SemaphoreType.DMA((3,)),
        ],
    )(x_groups, grad_groups, filters)
    got = lax.all_to_all(send, "seq", 0, 0, tiled=True)
    back = pl.pallas_call(
        conv_kernel,
        out_shape=coded,
        in_specs=[pl.BlockSpec(memory_space=pl.ANY), vmem],
        out_specs=vmem,
        scratch_shapes=[
            pltpu.VMEM((total, part, rows), jnp.bfloat16),
            pltpu.VMEM((total + 1, part, rows), jnp.float32),
            pltpu.VMEM((2, rows // 16, total * 16 // rows, part, rows), jnp.float32),
            pltpu.VMEM((part, 2 * total, rows), jnp.float32),
            pltpu.VMEM((UNROLL, 16 * total, rows), jnp.bfloat16),
            pltpu.VMEM((UNROLL, 2 * rows, 16 * total), jnp.bfloat16),
            pltpu.SMEM((total,), jnp.int32),
            pltpu.SemaphoreType.DMA,
        ],
        compiler_params=params,
    )(group_order, got)
    home = lax.all_to_all(back, "seq", 0, 0, tiled=True)
    grad_x, grad_filters = pl.pallas_call(
        unpack_kernel,
        out_shape=(
            jax.ShapeDtypeStruct((blocks, rows, channels), jnp.bfloat16),
            jax.ShapeDtypeStruct((blocks * rows, channels), jnp.float32),
        ),
        in_specs=[vmem],
        out_specs=(vmem, vmem),
        compiler_params=params,
    )(home)
    return grad_x, grad_filters


def solution(mesh):
    placed = (P("seq", None, "chan"), P("seq", None, "chan"), P("seq", "chan"), P())
    return jax.shard_map(
        per_device,
        mesh=mesh,
        in_specs=placed,
        out_specs=(P("seq", None, "chan"), P("seq", "chan")),
        check_vma=False,
    )
```

```python
import functools

import jax
import jax.numpy as jnp
from jax import lax
from jax.experimental import pallas as pl
from jax.experimental.pallas import tpu as pltpu
from jax.sharding import PartitionSpec as P

VMEM_LIMIT = 48 * 1024 * 1024
UNROLL = 16
CODE_SCALE = 2.0**30


def permuter(size, flip):
    rows = lax.broadcasted_iota(jnp.int32, (size, size), 0)
    cols = lax.broadcasted_iota(jnp.int32, (size, size), 1)
    if flip:
        cols = size - 1 - cols
    return (rows == cols).astype(jnp.float32).astype(jnp.bfloat16)


def transposed(eye, value):
    return lax.dot_general(
        eye, value, (((1,), (1,)), ((), ())), preferred_element_type=jnp.float32
    )


def pack_kernel(x_hbm, g_hbm, h_hbm, out_ref, x_ref, g_ref, h_ref, sems):
    peers, _, blocks, part, rows = out_ref.shape
    channels = peers * part
    copies = [
        pltpu.make_async_copy(source, target, sems.at[i])
        for i, (source, target) in enumerate(
            ((g_hbm, g_ref), (x_hbm, x_ref), (h_hbm, h_ref))
        )
    ]
    for copy in copies:
        copy.start()

    def put(a, b, value):
        out_ref[:, a, b] = value.astype(jnp.bfloat16).reshape(peers, part, rows)

    copies[0].wait()
    for b in range(blocks):
        put(1, b, g_ref[b].T)
    copies[1].wait()
    for b in range(blocks):
        put(0, b, x_ref[b].T)
    copies[2].wait()
    for b in range(blocks):
        put(2, b, h_ref[b * rows : (b + 1) * rows, :].T)


def unpack_kernel(in_ref, gx_ref, gf_ref):
    peers, _, blocks, part, rows = in_ref.shape
    channels = peers * part
    eye = permuter(rows, True)
    for b in range(blocks):
        cube = transposed(eye, in_ref[:, 0, b].reshape(channels, rows))
        dx = in_ref[:, 1, b].reshape(channels, rows)
        size = jnp.exp2(jnp.log2(jnp.abs(cube)) * (1.0 / 3.0)) * (1.0 / CODE_SCALE)
        size = jnp.where(cube == 0.0, 0.0, size)
        gf_ref[b * rows : (b + 1) * rows, :] = jnp.where(cube < 0.0, -size, size)
        gx_ref[b] = transposed(eye, dx).astype(jnp.bfloat16)


def conv_kernel(order_any, in_ref, out_ref, xs, seq, ub, res, wbuf, abuf, order_ref, order_sem):
    f32, bf16 = jnp.float32, jnp.bfloat16
    peers, _, blocks, part, rows = in_ref.shape
    total = peers * blocks
    order_copy = pltpu.make_async_copy(order_any, order_ref, order_sem)
    order_copy.start()
    fine = 16
    coarse = rows // fine
    groups = total // coarse

    def lane(shape):
        return lax.broadcasted_iota(jnp.int32, shape, 1)

    def row(shape):
        return lax.broadcasted_iota(jnp.int32, shape, 0)

    chunk = lane((part, rows)) // fine
    def regroup(v):
        for g in range(groups):
            tiles = []
            for i in range(coarse):
                k = g * coarse + i
                t = xs[k] if v == 0 else in_ref[k // blocks, 2, k % blocks]
                tiles.append(t)
            d = 1
            while d < coarse:
                odd = (chunk // d) % 2 == 1
                for i in range(coarse):
                    if (i // d) % 2 == 0:
                        a, b = tiles[i], tiles[i + d]
                        tiles[i] = jnp.where(odd, pltpu.roll(b, fine * d, 1), a)
                        tiles[i + d] = jnp.where(odd, b, pltpu.roll(a, rows - fine * d, 1))
                d *= 2
            for e in range(coarse):
                ub[v, e, g] = tiles[e].astype(f32)
    upper = lane((fine, rows)) >= row((fine, rows))
    stair = lane((coarse, rows)) >= fine * row((coarse, rows))
    lanes = lane((fine, rows))
    last = row((2 * fine, rows)) == 2 * fine - 1
    def prepare_right(c, slot):
        def slanted(k):
            line = jnp.broadcast_to(seq[k, pl.ds(c, 1), :], (fine, rows)).astype(bf16)
            return pltpu.roll(line, 0, 1, stride=1, stride_axis=0)
        now = slanted(0)
        for k in range(total):
            after = slanted(k + 1) if k + 1 < total else jnp.zeros((fine, rows), bf16)
            wbuf[slot, k * fine : (k + 1) * fine, :] = jnp.where(upper, now, after)
            now = after
    def prepare_left(c, slot, v):
        for e in range(coarse):
            before = jnp.zeros((coarse, rows), f32)
            shifted = [before]
            for g in range(groups):
                line = jnp.broadcast_to(ub[v, e, g, pl.ds(c, 1), :], (coarse, rows))
                turned = pltpu.roll(line, 0, 1, stride=fine, stride_axis=0)
                shifted.append(jnp.where(stair, turned, before))
                before = turned
            at = (2 * e + v) * fine
            for g in range(groups):
                abuf[slot, at : at + fine, g * rows : (g + 1) * rows] = jnp.concatenate([shifted[g + 1], shifted[g]], axis=0).astype(bf16)
    def finish(c, slot):
        half_k = total // 2 * fine
        w1 = wbuf[slot, half_k:, :]
        first = jnp.dot(
            abuf[slot, :, : 2 * rows],
            jnp.concatenate([wbuf[slot, :half_k, :], w1], axis=1),
            preferred_element_type=f32,
        )
        second = jnp.dot(abuf[slot, :, 2 * rows :], w1, preferred_element_type=f32)
        low = first[:, :rows] + second
        high = first[:, rows:]
        for v in range(2):
            halves = []
            for half in (low, high):
                straight = half[v * fine : (v + 1) * fine]
                wrapped = jnp.zeros((fine, rows), f32)
                for e in range(1, coarse):
                    at = (2 * e + v) * fine
                    turned = pltpu.roll(half[at : at + fine], fine * e, 1)
                    keep = jnp.where(lanes >= fine * e, turned, 0.0)
                    straight += keep
                    wrapped += turned - keep
                halves.append((straight, wrapped))
            straight = jnp.concatenate([h[0] for h in halves], axis=0)
            wrapped = jnp.concatenate([h[1] for h in halves], axis=0)
            wrapped = jnp.where(last, 0.0, pltpu.roll(wrapped, 2 * fine - 1, 0))
            res[c, v * total : (v + 1) * total] = straight + wrapped

    regroup(1)
    for u in range(UNROLL):
        prepare_left(u, u, 1)
    flip = permuter(rows, True)
    grads = in_ref[:, 1].reshape(total * part, rows)
    flipped = jnp.dot(grads, flip, preferred_element_type=f32)
    order_copy.wait()
    for j in range(total):
        place = order_ref[j]
        xs[place] = in_ref[j // blocks, 0, j % blocks]
        seq[place] = flipped[j * part : (j + 1) * part]
    regroup(0)
    for first in range(0, part, UNROLL):
        for u in range(UNROLL):
            prepare_right(first + u, u)
            prepare_left(first + u, u, 0)
            if first:
                prepare_left(first + u, u, 1)
        for u in range(UNROLL):
            finish(first + u, u)
    results = res.reshape(part * 2 * total, rows)
    for j in range(total):
        place = order_ref[j]
        value = results[pl.ds(j, part, stride=2 * total), :]
        dx = results[pl.ds(total + place, part, stride=2 * total), :]
        value = value * CODE_SCALE
        out_ref[j // blocks, 0, j % blocks] = (value * value * value).astype(bf16)
        out_ref[j // blocks, 1, j % blocks] = dx.astype(bf16)


def per_device(x_groups, grad_groups, filters, group_order):
    blocks, rows, channels = x_groups.shape
    peers = lax.axis_size("seq")
    part = channels // peers
    total = peers * blocks
    vmem = pl.BlockSpec(memory_space=pltpu.VMEM)
    params = pltpu.CompilerParams(vmem_limit_bytes=VMEM_LIMIT)
    packed = jax.ShapeDtypeStruct((peers, 3, blocks, part, rows), jnp.bfloat16)
    coded = jax.ShapeDtypeStruct((peers, 2, blocks, part, rows), jnp.bfloat16)
    send = pl.pallas_call(
        pack_kernel,
        out_shape=packed,
        in_specs=[pl.BlockSpec(memory_space=pl.ANY)] * 3,
        out_specs=vmem,
        scratch_shapes=[
            pltpu.VMEM((blocks, rows, channels), jnp.bfloat16),
            pltpu.VMEM((blocks, rows, channels), jnp.bfloat16),
            pltpu.VMEM((blocks * rows, channels), jnp.bfloat16),
            pltpu.SemaphoreType.DMA((3,)),
        ],
    )(x_groups, grad_groups, filters)
    got = lax.all_to_all(send, "seq", 0, 0, tiled=True)
    back = pl.pallas_call(
        conv_kernel,
        out_shape=coded,
        in_specs=[pl.BlockSpec(memory_space=pl.ANY), vmem],
        out_specs=vmem,
        scratch_shapes=[
            pltpu.VMEM((total, part, rows), jnp.bfloat16),
            pltpu.VMEM((total + 1, part, rows), jnp.float32),
            pltpu.VMEM((2, rows // 16, total * 16 // rows, part, rows), jnp.float32),
            pltpu.VMEM((part, 2 * total, rows), jnp.float32),
            pltpu.VMEM((UNROLL, 16 * total, rows), jnp.bfloat16),
            pltpu.VMEM((UNROLL, 2 * rows, 16 * total), jnp.bfloat16),
            pltpu.SMEM((total,), jnp.int32),
            pltpu.SemaphoreType.DMA,
        ],
        compiler_params=params,
    )(group_order, got)
    home = lax.all_to_all(back, "seq", 0, 0, tiled=True)
    grad_x, grad_filters = pl.pallas_call(
        unpack_kernel,
        out_shape=(
            jax.ShapeDtypeStruct((blocks, rows, channels), jnp.bfloat16),
            jax.ShapeDtypeStruct((blocks * rows, channels), jnp.float32),
        ),
        in_specs=[vmem],
        out_specs=(vmem, vmem),
        compiler_params=params,
    )(home)
    return grad_x, grad_filters


def solution(mesh):
    placed = (P("seq", None, "chan"), P("seq", None, "chan"), P("seq", "chan"), P())
    return jax.shard_map(
        per_device,
        mesh=mesh,
        in_specs=placed,
        out_specs=(P("seq", None, "chan"), P("seq", "chan")),
        check_vma=False,
    )
```

```python
import functools

import jax
import jax.numpy as jnp
from jax import lax
from jax.experimental import pallas as pl
from jax.experimental.pallas import tpu as pltpu
from jax.sharding import PartitionSpec as P

VMEM_LIMIT = 48 * 1024 * 1024
UNROLL = 16
CODE_SCALE = 2.0**30


def permuter(size, flip):
    rows = lax.broadcasted_iota(jnp.int32, (size, size), 0)
    cols = lax.broadcasted_iota(jnp.int32, (size, size), 1)
    if flip:
        cols = size - 1 - cols
    return (rows == cols).astype(jnp.float32).astype(jnp.bfloat16)


def transposed(eye, value):
    return jnp.dot(eye, value.T, preferred_element_type=jnp.float32)


def pack_kernel(x_hbm, g_hbm, h_hbm, out_ref, x_ref, g_ref, h_ref, sems):
    peers, _, blocks, part, rows = out_ref.shape
    channels = peers * part
    copies = [
        pltpu.make_async_copy(source, target, sems.at[i])
        for i, (source, target) in enumerate(
            ((g_hbm, g_ref), (x_hbm, x_ref), (h_hbm, h_ref))
        )
    ]
    for copy in copies:
        copy.start()

    def put(a, b, value):
        out_ref[:, a, b] = value.astype(jnp.bfloat16).reshape(peers, part, rows)

    copies[0].wait()
    for b in range(blocks):
        put(1, b, g_ref[b].T)
    copies[1].wait()
    for b in range(blocks):
        put(0, b, x_ref[b].T)
    copies[2].wait()
    for b in range(blocks):
        put(2, b, h_ref[b * rows : (b + 1) * rows, :].T)


def unpack_kernel(in_ref, gx_ref, gf_ref):
    peers, _, blocks, part, rows = in_ref.shape
    channels = peers * part
    eye = permuter(rows, True)
    for b in range(blocks):
        cube = transposed(eye, in_ref[:, 0, b].reshape(channels, rows))
        dx = in_ref[:, 1, b].reshape(channels, rows)
        size = jnp.exp2(jnp.log2(jnp.abs(cube)) * (1.0 / 3.0)) * (1.0 / CODE_SCALE)
        size = jnp.where(cube == 0.0, 0.0, size)
        gf_ref[b * rows : (b + 1) * rows, :] = jnp.where(cube < 0.0, -size, size)
        gx_ref[b] = transposed(eye, dx).astype(jnp.bfloat16)


def conv_kernel(order_any, in_ref, out_ref, xs, seq, ub, res, wbuf, abuf, order_ref, order_sem):
    f32, bf16 = jnp.float32, jnp.bfloat16
    peers, _, blocks, part, rows = in_ref.shape
    total = peers * blocks
    order_copy = pltpu.make_async_copy(order_any, order_ref, order_sem)
    order_copy.start()
    fine = 16
    coarse = rows // fine
    groups = total // coarse

    def lane(shape):
        return lax.broadcasted_iota(jnp.int32, shape, 1)

    def row(shape):
        return lax.broadcasted_iota(jnp.int32, shape, 0)

    chunk = lane((part, rows)) // fine
    def regroup(v):
        for g in range(groups):
            tiles = []
            for i in range(coarse):
                k = g * coarse + i
                t = xs[k] if v == 0 else in_ref[k // blocks, 2, k % blocks]
                tiles.append(t.astype(f32))
            d = 1
            while d < coarse:
                odd = (chunk // d) % 2 == 1
                for i in range(coarse):
                    if (i // d) % 2 == 0:
                        a, b = tiles[i], tiles[i + d]
                        tiles[i] = jnp.where(odd, pltpu.roll(b, fine * d, 1), a)
                        tiles[i + d] = jnp.where(odd, b, pltpu.roll(a, rows - fine * d, 1))
                d *= 2
            for e in range(coarse):
                ub[v, e, g] = tiles[e]
    upper = lane((fine, rows)) >= row((fine, rows))
    stair = lane((coarse, rows)) >= fine * row((coarse, rows))
    lanes = lane((fine, rows))
    last = row((2 * fine, rows)) == 2 * fine - 1
    def prepare_right(c, slot):
        def slanted(k):
            line = jnp.broadcast_to(seq[k, pl.ds(c, 1), :], (fine, rows)).astype(bf16)
            return pltpu.roll(line, 0, 1, stride=1, stride_axis=0)
        now = slanted(0)
        for k in range(total):
            after = slanted(k + 1) if k + 1 < total else jnp.zeros((fine, rows), bf16)
            wbuf[slot, k * fine : (k + 1) * fine, :] = jnp.where(upper, now, after)
            now = after
    def prepare_left(c, slot, v):
        for e in range(coarse):
            before = jnp.zeros((coarse, rows), f32)
            shifted = [before]
            for g in range(groups):
                line = jnp.broadcast_to(ub[v, e, g, pl.ds(c, 1), :], (coarse, rows))
                turned = pltpu.roll(line, 0, 1, stride=fine, stride_axis=0)
                shifted.append(jnp.where(stair, turned, before))
                before = turned
            at = (2 * e + v) * fine
            for g in range(groups):
                abuf[slot, at : at + fine, g * rows : (g + 1) * rows] = jnp.concatenate([shifted[g + 1], shifted[g]], axis=0).astype(bf16)
    def finish(c, slot):
        half_k = total // 2 * fine
        w1 = wbuf[slot, half_k:, :]
        first = jnp.dot(
            abuf[slot, :, : 2 * rows],
            jnp.concatenate([wbuf[slot, :half_k, :], w1], axis=1),
            preferred_element_type=f32,
        )
        second = jnp.dot(abuf[slot, :, 2 * rows :], w1, preferred_element_type=f32)
        low = first[:, :rows] + second
        high = first[:, rows:]
        for v in range(2):
            halves = []
            for half in (low, high):
                straight = half[v * fine : (v + 1) * fine]
                wrapped = jnp.zeros((fine, rows), f32)
                for e in range(1, coarse):
                    at = (2 * e + v) * fine
                    turned = pltpu.roll(half[at : at + fine], fine * e, 1)
                    keep = jnp.where(lanes >= fine * e, turned, 0.0)
                    straight += keep
                    wrapped += turned - keep
                halves.append((straight, wrapped))
            straight = jnp.concatenate([h[0] for h in halves], axis=0)
            wrapped = jnp.concatenate([h[1] for h in halves], axis=0)
            wrapped = jnp.where(last, 0.0, pltpu.roll(wrapped, 2 * fine - 1, 0))
            res[c, v * total : (v + 1) * total] = straight + wrapped

    regroup(1)
    for u in range(UNROLL):
        prepare_left(u, u, 1)
    flip = permuter(rows, True)
    grads = in_ref[:, 1].reshape(total * part, rows)
    flipped = jnp.dot(grads, flip, preferred_element_type=f32)
    order_copy.wait()
    for j in range(total):
        place = order_ref[j]
        xs[place] = in_ref[j // blocks, 0, j % blocks]
        seq[place] = flipped[j * part : (j + 1) * part]
    regroup(0)
    for first in range(0, part, UNROLL):
        for u in range(UNROLL):
            prepare_right(first + u, u)
            prepare_left(first + u, u, 0)
            if first:
                prepare_left(first + u, u, 1)
        for u in range(UNROLL):
            finish(first + u, u)
    results = res.reshape(part * 2 * total, rows)
    for j in range(total):
        place = order_ref[j]
        value = results[pl.ds(j, part, stride=2 * total), :]
        dx = results[pl.ds(total + place, part, stride=2 * total), :]
        value = value * CODE_SCALE
        out_ref[j // blocks, 0, j % blocks] = (value * value * value).astype(bf16)
        out_ref[j // blocks, 1, j % blocks] = dx.astype(bf16)


def per_device(x_groups, grad_groups, filters, group_order):
    blocks, rows, channels = x_groups.shape
    peers = lax.axis_size("seq")
    part = channels // peers
    total = peers * blocks
    vmem = pl.BlockSpec(memory_space=pltpu.VMEM)
    params = pltpu.CompilerParams(vmem_limit_bytes=VMEM_LIMIT)
    packed = jax.ShapeDtypeStruct((peers, 3, blocks, part, rows), jnp.bfloat16)
    coded = jax.ShapeDtypeStruct((peers, 2, blocks, part, rows), jnp.bfloat16)
    send = pl.pallas_call(
        pack_kernel,
        out_shape=packed,
        in_specs=[pl.BlockSpec(memory_space=pl.ANY)] * 3,
        out_specs=vmem,
        scratch_shapes=[
            pltpu.VMEM((blocks, rows, channels), jnp.bfloat16),
            pltpu.VMEM((blocks, rows, channels), jnp.bfloat16),
            pltpu.VMEM((blocks * rows, channels), jnp.bfloat16),
            pltpu.SemaphoreType.DMA((3,)),
        ],
    )(x_groups, grad_groups, filters)
    got = lax.all_to_all(send, "seq", 0, 0, tiled=True)
    back = pl.pallas_call(
        conv_kernel,
        out_shape=coded,
        in_specs=[pl.BlockSpec(memory_space=pl.ANY), vmem],
        out_specs=vmem,
        scratch_shapes=[
            pltpu.VMEM((total, part, rows), jnp.bfloat16),
            pltpu.VMEM((total + 1, part, rows), jnp.float32),
            pltpu.VMEM((2, rows // 16, total * 16 // rows, part, rows), jnp.float32),
            pltpu.VMEM((part, 2 * total, rows), jnp.float32),
            pltpu.VMEM((UNROLL, 16 * total, rows), jnp.bfloat16),
            pltpu.VMEM((UNROLL, 2 * rows, 16 * total), jnp.bfloat16),
            pltpu.SMEM((total,), jnp.int32),
            pltpu.SemaphoreType.DMA,
        ],
        compiler_params=params,
    )(group_order, got)
    home = lax.all_to_all(back, "seq", 0, 0, tiled=True)
    grad_x, grad_filters = pl.pallas_call(
        unpack_kernel,
        out_shape=(
            jax.ShapeDtypeStruct((blocks, rows, channels), jnp.bfloat16),
            jax.ShapeDtypeStruct((blocks * rows, channels), jnp.float32),
        ),
        in_specs=[vmem],
        out_specs=(vmem, vmem),
        compiler_params=params,
    )(home)
    return grad_x, grad_filters


def solution(mesh):
    placed = (P("seq", None, "chan"), P("seq", None, "chan"), P("seq", "chan"), P())
    return jax.shard_map(
        per_device,
        mesh=mesh,
        in_specs=placed,
        out_specs=(P("seq", None, "chan"), P("seq", "chan")),
        check_vma=False,
    )
```
